32 devices in a mesh: groups: 2 (over y), expert: 4 (over z), tensor: 2 (over x), seq: 2 (over core).
Axes of the slice: x: 2, y: 2, z: 4, core: 2. Of those that a mesh axis runs over, the one named last changes fastest.
Arguments:
- tokens: bfloat16 [2048, 4096], P(('groups', 'expert'), 'seq'), parts along dimension 0, may hold values from -6 to 6
- gate_weight: bfloat16 [4, 4096, 768], P('expert', 'seq', 'tensor'), may hold values from -0.09375 to 0.09375
- up_weight: bfloat16 [4, 4096, 768], P('expert', 'seq', 'tensor'), may hold values from -0.09375 to 0.09375
- down_weight: bfloat16 [4, 768, 4096], P('expert', None, ('tensor', 'seq')), may hold values from -0.15625 to 0.15625
- expert_ids: int32 [2048, 1], P(('groups', 'expert')), parts along dimension 0, may hold values from 0 to 1; in each aligned block of 256 rows (0 to 255, 256 to 511, ...) at most 256 rows name the same one
- codes: int32 [2048, 1], P(('groups', 'expert')), parts along dimension 0, may hold values from 64 to 1024
- expert_home: int32 [2], replicated, may hold values from 0 to 1, each once
Outputs:
- mixed: bfloat16 [2048, 4096], P(('groups', 'expert'), ('tensor', 'seq')), parts along dimension 0
The draws below stay inside these ranges and needn't reach their ends.
There are 2 independent parts, one for each index of `groups`. The reference program is written for one: setup_inputs(seed, part) draws one part's arguments, and reference() takes and returns one part's arrays. A program takes and returns all parts, laid end to end along the dimension named above; an argument that names none is the same for every part. Nothing has to cross between parts.
Inputs may be any that keep to these rules, and one draw needn't show every extreme that they name: `expert_ids`: in each aligned block of 256 rows no expert is named by more than 256 rows, and in some block an expert is named by exactly 256 rows. `expert_home`: every slot is the home of exactly one expert.
All inputs are finite; a program needn't handle non-finite values.
Results may differ from the reference program's by a relative error of at most 0.0057.
Values may be sent and summed in bfloat16 or wider, within the bound.
No kernel may reach another device: no remote copies, remote signals or barrier semaphores. Data moves between devices by JAX's collectives and lax.ppermute only.
A program may use at most 64 MiB of HBM per device.

```python
import math
import jax
import jax.numpy as jnp
import numpy as np
from jax import lax

D = 4096
FF = 1536
TOK_DEV = 256
TOP = 1
EXPERTS = 2
CAP = 256
TOKENS = 1024
N_EXPERT = 4


def set_ends(result, key, low, high):
    shape = result.shape
    index_at = [jax.random.randint(jax.random.fold_in(key, axis), (), 0, shape[axis]) for axis in range(len(shape))]
    result = result.at[tuple(index_at)].set(low)
    longest = shape.index(max(shape))
    index_at[longest] = (index_at[longest] + 1) % shape[longest]
    return result.at[tuple(index_at)].set(high)


def block_levels(stream_key, extent, cuts, smallest, high):
    loudness, own = 1.0, jax.random.fold_in(stream_key, 6)
    for dim, blocks in cuts:
        heights = jnp.exp(jax.random.uniform(jax.random.fold_in(own, dim), (blocks,), jnp.float32, smallest / len(cuts), high / len(cuts)))
        loudness = loudness * jnp.repeat(heights, extent[dim] // blocks).reshape([-1 if axis == dim else 1 for axis in range(len(extent))])
    return loudness


def shared_out(stream_key, own, number, rows, amount, top, bound, skew):
    sequence = jax.random.permutation(stream_key, amount)
    packed, ordinary = load_shares(amount, rows * top, bound, skew, True), load_shares(amount, rows * top, bound, skew, False)
    places = jnp.arange(amount)

    def named(sizes, rotation):
        used = int((sizes > 0).sum())
        fixed = max(1, used // 4)
        shifted = fixed + (places - fixed + rotation * (used - fixed)) % max(1, amount - fixed)
        return jnp.zeros((amount,), jnp.int32).at[sequence[jnp.where(places < fixed, places, shifted)]].set(jnp.asarray(sizes, jnp.int32))

    sizes = jnp.where(number % 4 == 0, named(packed, number // 4), named(ordinary, number - number // 4 - 1))
    mixed = jax.random.permutation(jax.random.fold_in(own, 3), amount)
    source_of, receiver = mixed[0:amount // 2 * 2:2], mixed[1:amount // 2 * 2:2]
    margin = jnp.minimum(sizes[source_of] - 1, bound - sizes[receiver]) // 2
    margin = jnp.where((source_of == sequence[0]) | (receiver == sequence[0]) | (sizes[receiver] == 0), 0, jnp.maximum(margin, 0))
    shifted = jax.random.randint(jax.random.fold_in(own, 4), (amount // 2,), 0, 1 << 20) % (margin + 1)
    sizes = sizes.at[source_of].add(-shifted).at[receiver].add(shifted)
    members = jnp.searchsorted(jnp.cumsum(sizes), jnp.arange(rows * top), side="right").astype(jnp.int32)
    listing = members.reshape(top, rows).T
    listing = listing[jax.random.permutation(jax.random.fold_in(own, 1), rows)]
    rotation = jax.random.randint(jax.random.fold_in(own, 2), (rows, 1), 0, top)
    return jnp.take_along_axis(listing, (jnp.arange(top)[None, :] + rotation) % top, axis=1)


def load_shares(count, total, reach, lean, full):
    weights = [(1 << 20) // math.isqrt(standing ** lean) + 1 for standing in range(1, count + 1)]
    largest = reach if full else min(reach, max(-(-total // count), total * weights[0] // sum(weights)))
    least = 1 if total - largest >= count - 1 else 0
    holding, rest = [largest] + [least] * (count - 1), total - largest - least * (count - 1)
    while rest > 0:
        free = [i for i in range(1, count) if holding[i] < largest] or [i for i in range(1, count) if holding[i] < reach]
        whole, budget = sum([weights[i] for i in free]), rest
        for i in free:
            extra = min(reach - holding[i], max(1, budget * weights[i] // whole), rest)
            holding[i] = holding[i] + extra
            rest = rest - extra
    return np.array(holding)


def normal_values(own_key, dims, deviation, bound, pieces=(), kind=jnp.bfloat16):
    level = block_levels(own_key, dims, pieces, -0.22, 0.18) if pieces else 1.0
    values = jax.random.normal(own_key, dims, jnp.float32) * deviation * level
    return jnp.minimum(jnp.maximum(values, -bound), bound).astype(kind)


def setup_inputs(seed: int = 0, part: int = 0) -> dict:
    keys = jax.random.split(jax.random.key(seed), 8)
    part_splits = jax.random.split(jax.random.fold_in(keys[7], part), 8)
    tokens = normal_values(part_splits[0], (TOKENS, D), 1.0, 6.0, ((0, 4), (1, 2)))
    gate_weight = normal_values(keys[1], (2 * EXPERTS, D, FF // 2), D ** -0.5, 0.09375, ((0, 4), (1, 2), (2, 2)))
    up_weight = normal_values(keys[2], (2 * EXPERTS, D, FF // 2), D ** -0.5, 0.09375, ((0, 4), (1, 2), (2, 2)))
    down_weight = normal_values(keys[3], (2 * EXPERTS, FF // 2, D), FF ** -0.5, 0.15625, ((0, 4), (2, 4)))
    expert_ids_keys = jax.random.split(jax.random.fold_in(part_splits[4], 1), TOKENS // TOK_DEV)
    expert_ids_turns = jax.random.permutation(jax.random.fold_in(part_splits[4], 3), TOKENS // TOK_DEV)
    expert_ids = jax.vmap(lambda own, number: shared_out(jax.random.fold_in(part_splits[4], 2), own, number, TOK_DEV, EXPERTS, TOP, CAP, 2))(expert_ids_keys, expert_ids_turns).reshape((TOKENS, TOP))
    codes = set_ends(jax.random.randint(part_splits[5], (TOKENS, TOP), 64, 1025), jax.random.fold_in(part_splits[5], 1), 64, 1024).astype(jnp.int32)
    expert_home = jax.random.permutation(keys[6], EXPERTS).astype(jnp.int32)
    return dict(tokens=tokens, gate_weight=gate_weight, up_weight=up_weight, down_weight=down_weight, expert_ids=expert_ids, codes=codes, expert_home=expert_home)


def reference(tokens, gate_weight, up_weight, down_weight, expert_ids, codes, expert_home):
    home_slot = expert_home[expert_ids[:, 0]].astype(jnp.int32)
    scale = codes[:, 0].astype(jnp.float32) / 1024.0
    ordering = jnp.argsort(home_slot, stable=True).astype(jnp.int32)
    most_rows = N_EXPERT * CAP
    padded = jnp.concatenate([ordering, jnp.zeros((most_rows,), jnp.int32)])
    numbers = jnp.arange(EXPERTS, dtype=jnp.int32)
    counts = jnp.sum((home_slot[None, :] == numbers[:, None]).astype(jnp.int32), axis=1).astype(jnp.int32)
    starts = (jnp.cumsum(counts) - counts).astype(jnp.int32)

    def one_slot(slot_id):
        chosen = lax.dynamic_slice_in_dim(padded, starts[slot_id], most_rows)
        usable = jnp.arange(most_rows, dtype=jnp.int32) < counts[slot_id]
        selected = tokens[chosen]
        gate_full = jnp.concatenate([gate_weight[2 * slot_id], gate_weight[2 * slot_id + 1]], axis=1)
        up_full = jnp.concatenate([up_weight[2 * slot_id], up_weight[2 * slot_id + 1]], axis=1)
        down_full = jnp.concatenate([down_weight[2 * slot_id], down_weight[2 * slot_id + 1]], axis=0)
        gate_act = jnp.dot(selected, gate_full, preferred_element_type=jnp.float32)
        up_act = jnp.dot(selected, up_full, preferred_element_type=jnp.float32)
        hidden = (jax.nn.silu(gate_act) * up_act).astype(jnp.bfloat16)
        result_rows = jnp.dot(hidden, down_full, preferred_element_type=jnp.float32).astype(jnp.bfloat16)
        return jnp.where(usable[:, None], result_rows, jnp.zeros_like(result_rows)), chosen

    results, chosen_rows = lax.map(one_slot, numbers)
    expert_out = jnp.zeros(tokens.shape, jnp.bfloat16)
    expert_out = expert_out.at[chosen_rows.reshape(-1)].add(results.reshape(-1, tokens.shape[1]))
    return (scale[:, None] * expert_out.astype(jnp.float32)).astype(jnp.bfloat16)
```

```python
import jax
import jax.numpy as jnp
from jax import lax
from jax.sharding import PartitionSpec as P


def swapped(x, axis, distance):
    return lax.ppermute(x, axis, [(i, i ^ 1 << distance) for i in range(lax.axis_size(axis))])


def routed(tokens, gate_weight, up_weight, down_weight, expert_ids, codes, expert_home):
    tok_rows, columns_dev = tokens.shape
    experts = expert_home.shape[0]
    capacity = min(tok_rows, 2 * tok_rows // experts)
    owners = 2 * experts
    numbers = jnp.arange(experts, dtype=jnp.int32)
    chosen = (expert_ids == numbers[None, :]).astype(jnp.int32)
    home_slot = jnp.sum(chosen * expert_home[None, :], axis=1)
    onehot = (home_slot[:, None] == numbers[None, :]).astype(jnp.int32)
    before = jnp.cumsum(onehot, axis=0) - onehot
    position = jnp.sum(before * onehot, axis=1)
    target = home_slot * capacity + position
    select = (jnp.arange(experts * capacity, dtype=jnp.int32)[:, None] == target[None, :]).astype(
        jnp.bfloat16
    )
    packed = jnp.dot(select, tokens, preferred_element_type=jnp.float32).astype(jnp.bfloat16)
    packed = packed.reshape(experts, capacity, columns_dev)
    member = lax.axis_index("expert") % 2
    doubled = jnp.broadcast_to(packed[:, None], (experts, 2, capacity, columns_dev))
    doubled = doubled.reshape(owners, capacity, columns_dev)
    arrived = lax.all_to_all(doubled, "expert", split_axis=0, concat_axis=0, tiled=True)
    slot_count = owners * capacity
    received = arrived.reshape(slot_count, columns_dev)
    gate_part = jnp.dot(received, gate_weight[0], preferred_element_type=jnp.float32)
    up_part = jnp.dot(received, up_weight[0], preferred_element_type=jnp.float32)
    gate_act, up_act = lax.psum((gate_part, up_part), "seq")
    activated = (jax.nn.silu(gate_act) * up_act).astype(jnp.bfloat16)
    down_block = down_weight[0]
    out_columns = down_block.shape[1]
    partial_value = jnp.dot(
        lax.all_gather(activated, "tensor", axis=1, tiled=True),
        down_block,
        preferred_element_type=jnp.float32,
    )
    partial_value = partial_value.reshape(owners, capacity, out_columns)
    kept_rows = capacity // 2
    own_part = lax.dynamic_slice_in_dim(partial_value, member * kept_rows, kept_rows, 1)
    handed = lax.dynamic_slice_in_dim(partial_value, (1 - member) * kept_rows, kept_rows, 1)
    summed = own_part + swapped(handed, "expert", 0)
    returned = lax.all_to_all(
        summed.astype(jnp.bfloat16), "expert", split_axis=0, concat_axis=0, tiled=True
    )
    returned = returned.reshape(experts * capacity, out_columns)
    gathered = jnp.einsum("pt,pd->td", select, returned, preferred_element_type=jnp.float32)
    weights = codes[:, 0].astype(jnp.float32) / 1024.0
    return (weights[:, None] * gathered).astype(jnp.bfloat16)


PAIR = [(0, 1), (1, 0), (2, 3), (3, 2)]
ACROSS = [(1, 2), (2, 1)]
OUTWARD = [(1, 0), (2, 3)]
INWARD = [(0, 1), (3, 2)]
FAR = [(1, 3), (2, 0)]


def z_send(x, pairs):
    return lax.ppermute(x, "expert", pairs)


def half(x, index):
    rows = x.shape[0] // 2
    return lax.dynamic_slice_in_dim(x, index * rows, rows, 0)


def in_order(own, other, index):
    return jnp.where(index == 0, jnp.concatenate([own, other]), jnp.concatenate([other, own]))


def gathered_pairs(tokens, gate_weight, up_weight, down_weight, expert_ids, codes, expert_home):
    z, x, c = lax.axis_index("expert"), lax.axis_index("tensor"), lax.axis_index("seq")
    inner = (z == 1) | (z == 2)
    f32, bf16 = jnp.float32, jnp.bfloat16

    other_columns = swapped(half(tokens, 1 - c), "seq", 0)
    own_rows = jnp.concatenate([half(tokens, c), other_columns], axis=1)
    quarter = half(own_rows, x)

    from_pair = z_send(quarter, PAIR)
    from_across = z_send(quarter, ACROSS)
    weights = jnp.concatenate([gate_weight[0], up_weight[0]], axis=1)
    weights = jnp.concatenate([weights, swapped(weights, "seq", 0)], axis=0)
    down = down_weight[0]

    near = jnp.where(inner, from_across, z_send(from_across, OUTWARD))
    across_pair = z_send(from_pair, ACROSS)
    far = jnp.where(inner, across_pair, z_send(across_pair, OUTWARD))

    def with_tensor(part):
        return in_order(part, swapped(part, "tensor", 0), x)

    def hidden(rows):
        acts = jnp.dot(rows, weights, preferred_element_type=f32)
        gate_act, up_act = jnp.split(acts, 2, axis=1)
        own = (jax.nn.silu(gate_act) * up_act).astype(bf16)
        other = swapped(own, "tensor", 0)
        both = jnp.where(
            x == 0,
            jnp.concatenate([own, other], axis=1),
            jnp.concatenate([other, own], axis=1),
        )
        return in_order(both, swapped(both, "seq", 0), c)

    def partial_out(rows):
        return jnp.dot(hidden(rows), down, preferred_element_type=f32)

    own_part = partial_out(own_rows)
    pair_part = z_send(partial_out(with_tensor(from_pair)).astype(bf16), PAIR)
    near_part = partial_out(with_tensor(near))
    near_sum = near_part + z_send(near_part.astype(bf16), INWARD).astype(f32)
    returned = z_send(near_sum.astype(bf16), ACROSS)
    far_part = partial_out(with_tensor(far))
    far_sum = far_part + z_send(far_part.astype(bf16), INWARD).astype(f32)
    returned_far = z_send(far_sum.astype(bf16), FAR)

    ids = expert_ids[:, 0]
    home = jnp.where(ids == 0, expert_home[0], expert_home[1])
    ours = (home == z // 2)[:, None]
    local = (own_part + pair_part.astype(f32)).astype(bf16)
    expert_out = jnp.where(ours, local, jnp.where(inner, returned, returned_far))
    scale = codes[:, 0].astype(f32) / 1024.0
    return (scale[:, None] * expert_out.astype(f32)).astype(bf16)


def local(*arguments):
    experts = arguments[-1].shape[0]
    sizes = tuple(lax.axis_size(axis) for axis in ("expert", "tensor", "seq"))
    if experts == 2 and sizes == (4, 2, 2):
        return gathered_pairs(*arguments)
    return routed(*arguments)


def solution(mesh):
    in_specs = (
        P(("groups", "expert"), "seq"),
        P("expert", "seq", "tensor"),
        P("expert", "seq", "tensor"),
        P("expert", None, ("tensor", "seq")),
        P(("groups", "expert"), None),
        P(("groups", "expert"), None),
        P(),
    )
    out_specs = P(("groups", "expert"), ("tensor", "seq"))
    return jax.shard_map(local, mesh=mesh, in_specs=in_specs, out_specs=out_specs, check_vma=False)
```

```python
import functools

import jax
import jax.numpy as jnp
from jax import lax
from jax.experimental import pallas as pl
from jax.experimental.pallas import tpu as pltpu
from jax.sharding import PartitionSpec as P


def swapped(x, axis, distance):
    return lax.ppermute(x, axis, [(i, i ^ 1 << distance) for i in range(lax.axis_size(axis))])


def routed(tokens, gate_weight, up_weight, down_weight, expert_ids, codes, expert_home):
    tok_rows, columns_dev = tokens.shape
    experts = expert_home.shape[0]
    capacity = min(tok_rows, 2 * tok_rows // experts)
    owners = 2 * experts
    numbers = jnp.arange(experts, dtype=jnp.int32)
    chosen = (expert_ids == numbers[None, :]).astype(jnp.int32)
    home_slot = jnp.sum(chosen * expert_home[None, :], axis=1)
    onehot = (home_slot[:, None] == numbers[None, :]).astype(jnp.int32)
    before = jnp.cumsum(onehot, axis=0) - onehot
    position = jnp.sum(before * onehot, axis=1)
    target = home_slot * capacity + position
    select = (jnp.arange(experts * capacity, dtype=jnp.int32)[:, None] == target[None, :]).astype(
        jnp.bfloat16
    )
    packed = jnp.dot(select, tokens, preferred_element_type=jnp.float32).astype(jnp.bfloat16)
    packed = packed.reshape(experts, capacity, columns_dev)
    member = lax.axis_index("expert") % 2
    doubled = jnp.broadcast_to(packed[:, None], (experts, 2, capacity, columns_dev))
    doubled = doubled.reshape(owners, capacity, columns_dev)
    arrived = lax.all_to_all(doubled, "expert", split_axis=0, concat_axis=0, tiled=True)
    slot_count = owners * capacity
    received = arrived.reshape(slot_count, columns_dev)
    gate_part = jnp.dot(received, gate_weight[0], preferred_element_type=jnp.float32)
    up_part = jnp.dot(received, up_weight[0], preferred_element_type=jnp.float32)
    gate_act, up_act = lax.psum((gate_part, up_part), "seq")
    activated = (jax.nn.silu(gate_act) * up_act).astype(jnp.bfloat16)
    down_block = down_weight[0]
    out_columns = down_block.shape[1]
    partial_value = jnp.dot(
        lax.all_gather(activated, "tensor", axis=1, tiled=True),
        down_block,
        preferred_element_type=jnp.float32,
    )
    partial_value = partial_value.reshape(owners, capacity, out_columns)
    kept_rows = capacity // 2
    own_part = lax.dynamic_slice_in_dim(partial_value, member * kept_rows, kept_rows, 1)
    handed = lax.dynamic_slice_in_dim(partial_value, (1 - member) * kept_rows, kept_rows, 1)
    summed = own_part + swapped(handed, "expert", 0)
    returned = lax.all_to_all(
        summed.astype(jnp.bfloat16), "expert", split_axis=0, concat_axis=0, tiled=True
    )
    returned = returned.reshape(experts * capacity, out_columns)
    gathered = jnp.einsum("pt,pd->td", select, returned, preferred_element_type=jnp.float32)
    weights = codes[:, 0].astype(jnp.float32) / 1024.0
    return (weights[:, None] * gathered).astype(jnp.bfloat16)


def z_send(x, distance):
    size = lax.axis_size("expert")
    return lax.ppermute(x, "expert", [(i, i ^ distance) for i in range(size)])


def ring_send(x):
    size, cores = lax.axis_size("expert"), lax.axis_size("seq")
    pairs = [
        (i * cores + core, (i + step) % size * cores + core)
        for i in range(size)
        for core, step in enumerate((1, -1))
    ]
    return lax.ppermute(x, ("expert", "seq"), pairs)


def half(x, index):
    rows = x.shape[0] // 2
    return lax.dynamic_slice_in_dim(x, index * rows, rows, 0)


def in_order(own, other, index, axis=0):
    return jnp.where(
        index == 0,
        jnp.concatenate([own, other], axis),
        jnp.concatenate([other, own], axis),
    )


VMEM = pl.BlockSpec(memory_space=pltpu.VMEM)
SMEM = pl.BlockSpec(memory_space=pltpu.SMEM)
LIMIT = 16 * 1024 * 1024


def hidden_kernel(parts, index, *refs):
    taken, weights, (out, acts) = refs[: 2 * parts], refs[2 * parts : -2], refs[-2:]
    rows, depth = out.shape[0] // 2, weights[0].shape[0]
    width = out.shape[1]
    step = 1024
    for i in range(2 * depth // step):
        pair, start = divmod(i * step, depth)
        block = jnp.concatenate(
            [ref[pl.ds(start, step), :] for ref in weights[2 * pair : 2 * pair + 2]], axis=1
        )
        value = jnp.dot(
            jnp.concatenate([ref[:, pl.ds(i * step, step)] for ref in taken], axis=0),
            block,
            preferred_element_type=jnp.float32,
        )
        if i == 0:
            acts[...] = value
        else:
            acts[...] += value

    gate_act, up_act = acts[:, :width], acts[:, width:]
    value = (jax.nn.silu(gate_act) * up_act).astype(out.dtype)
    place = index[0]
    out[pl.ds(pl.multiple_of(place * rows, rows), rows), :] = value[:rows]
    out[pl.ds(pl.multiple_of((1 - place) * rows, rows), rows), :] = value[rows:]


def hidden_call(index, first, second, weights):
    rows, width = sum(part.shape[0] for part in first), weights[0].shape[1]
    operands = (*first, *second, *weights)
    return pl.pallas_call(
        functools.partial(hidden_kernel, len(first)),
        out_shape=jax.ShapeDtypeStruct((2 * rows, width), jnp.bfloat16),
        in_specs=[SMEM] + [VMEM] * len(operands),
        out_specs=VMEM,
        scratch_shapes=[pltpu.VMEM((2 * rows, 2 * width), jnp.float32)],
        compiler_params=pltpu.CompilerParams(vmem_limit_bytes=LIMIT),
        cost_estimate=pl.CostEstimate(
            flops=0,
            bytes_accessed=0,
            transcendentals=0,
        ),
    )(index, *operands)


def ring(tokens, gate_weight, up_weight, down_weight, expert_ids, codes, expert_home):
    z, x, c = lax.axis_index("expert"), lax.axis_index("tensor"), lax.axis_index("seq")
    f32, bf16 = jnp.float32, jnp.bfloat16
    tied = lax.optimization_barrier
    odd = z % 2
    place = c ^ odd
    x_index = x.astype(jnp.int32).reshape(1)

    def to_tensor(part):
        return swapped(part, "tensor", 0)

    down = down_weight[0]
    own_half, given_half = half(tokens, c), half(tokens, 1 - c)
    own_rows = tied(jnp.concatenate([own_half, swapped(given_half, "seq", 0)], axis=1))
    moving, staying = tied((half(own_rows, x), half(own_rows, 1 - x)))
    block1 = ring_send(moving)
    gate_own, up_own, staying = tied((gate_weight[0], up_weight[0], staying))
    weights = (gate_own, up_own, swapped(gate_own, "seq", 0), swapped(up_own, "seq", 0))

    def activated(part, other):
        return hidden_call(x_index, (part,), (other,), weights)

    def partial_out(own, other):
        both = in_order(own, other, x, 1)
        rows = in_order(both, swapped(both, "seq", 0), place)
        return jnp.dot(rows, down, preferred_element_type=f32)

    def a_half(part):
        return part[: part.shape[0] // 2]

    def b_half(part):
        return part[part.shape[0] // 2 :]

    def added(part, received):
        return (part + received.astype(f32)).astype(bf16)

    act0 = activated(moving, staying)
    hidden0 = to_tensor(act0)
    block1, act0, hidden0 = tied((block1, act0, hidden0))
    block2, other1 = ring_send(block1), to_tensor(block1)
    part0 = partial_out(act0, hidden0)
    block2, other1, part0 = tied((block2, other1, part0))
    block3, other2 = ring_send(block2), to_tensor(block2)
    act1 = activated(block1, other1)
    hidden1 = to_tensor(act1)
    block3, other2, hidden1 = tied((block3, other2, hidden1))
    other3 = to_tensor(block3)
    part1 = partial_out(act1, hidden1).astype(bf16)
    back1 = z_send(part1, 1)
    act2 = activated(block2, other2)
    hidden2 = to_tensor(act2)
    other3, part1, hidden2 = tied((other3, part1, hidden2))
    part2 = partial_out(act2, hidden2)
    act3 = activated(block3, other3)
    back1, part2, act3 = tied((back1, part2, act3))
    sent_a2 = z_send(a_half(part2).astype(bf16), 1)
    home_b2 = z_send(added(b_half(part2), a_half(back1)), 2)
    part3 = partial_out(act3, to_tensor(act3))
    sent_a3 = z_send(a_half(part3).astype(bf16), 1)
    sent_a2, home_b2, part3 = tied((sent_a2, home_b2, part3))
    home_b3 = z_send(added(b_half(part3), sent_a2), 3)

    def in_rows(part_a, part_b):
        return in_order(part_a, part_b, odd)

    ids = expert_ids[:, 0]
    home = jnp.where(ids == 0, expert_home[0], expert_home[1])
    ours = (home == z // 2)[:, None]
    scale = codes[:, 0].astype(f32) / 1024.0
    from_pair = in_rows(
        a_half(part0) + b_half(back1).astype(f32), b_half(part0) + sent_a3.astype(f32)
    )
    from_others = in_rows(home_b3, home_b2).astype(f32)
    expert_out = jnp.where(ours, from_pair, from_others).astype(bf16)
    return (scale[:, None] * expert_out.astype(f32)).astype(bf16)


def local(*arguments):
    experts = arguments[-1].shape[0]
    sizes = tuple(lax.axis_size(axis) for axis in ("expert", "tensor", "seq"))
    if experts == 2 and sizes == (4, 2, 2):
        return ring(*arguments)
    return routed(*arguments)


def solution(mesh):
    in_specs = (
        P(("groups", "expert"), "seq"),
        P("expert", "seq", "tensor"),
        P("expert", "seq", "tensor"),
        P("expert", None, ("tensor", "seq")),
        P(("groups", "expert"), None),
        P(("groups", "expert"), None),
        P(),
    )
    out_specs = P(("groups", "expert"), ("tensor", "seq"))
    return jax.shard_map(local, mesh=mesh, in_specs=in_specs, out_specs=out_specs, check_vma=False)
```

```python
import functools

import jax
import jax.numpy as jnp
from jax import lax
from jax.experimental import pallas as pl
from jax.experimental.pallas import tpu as pltpu
from jax.sharding import PartitionSpec as P


def swapped(x, axis, distance):
    return lax.ppermute(x, axis, [(i, i ^ 1 << distance) for i in range(lax.axis_size(axis))])


def routed(tokens, gate_weight, up_weight, down_weight, expert_ids, codes, expert_home):
    tok_rows, columns_dev = tokens.shape
    experts = expert_home.shape[0]
    capacity = min(tok_rows, 2 * tok_rows // experts)
    owners = 2 * experts
    numbers = jnp.arange(experts, dtype=jnp.int32)
    chosen = (expert_ids == numbers[None, :]).astype(jnp.int32)
    home_slot = jnp.sum(chosen * expert_home[None, :], axis=1)
    onehot = (home_slot[:, None] == numbers[None, :]).astype(jnp.int32)
    before = jnp.cumsum(onehot, axis=0) - onehot
    position = jnp.sum(before * onehot, axis=1)
    target = home_slot * capacity + position
    select = (jnp.arange(experts * capacity, dtype=jnp.int32)[:, None] == target[None, :]).astype(
        jnp.bfloat16
    )
    packed = jnp.dot(select, tokens, preferred_element_type=jnp.float32).astype(jnp.bfloat16)
    packed = packed.reshape(experts, capacity, columns_dev)
    member = lax.axis_index("expert") % 2
    doubled = jnp.broadcast_to(packed[:, None], (experts, 2, capacity, columns_dev))
    doubled = doubled.reshape(owners, capacity, columns_dev)
    arrived = lax.all_to_all(doubled, "expert", split_axis=0, concat_axis=0, tiled=True)
    slot_count = owners * capacity
    received = arrived.reshape(slot_count, columns_dev)
    gate_part = jnp.dot(received, gate_weight[0], preferred_element_type=jnp.float32)
    up_part = jnp.dot(received, up_weight[0], preferred_element_type=jnp.float32)
    gate_act, up_act = lax.psum((gate_part, up_part), "seq")
    activated = (jax.nn.silu(gate_act) * up_act).astype(jnp.bfloat16)
    down_block = down_weight[0]
    out_columns = down_block.shape[1]
    partial_value = jnp.dot(
        lax.all_gather(activated, "tensor", axis=1, tiled=True),
        down_block,
        preferred_element_type=jnp.float32,
    )
    partial_value = partial_value.reshape(owners, capacity, out_columns)
    kept_rows = capacity // 2
    own_part = lax.dynamic_slice_in_dim(partial_value, member * kept_rows, kept_rows, 1)
    handed = lax.dynamic_slice_in_dim(partial_value, (1 - member) * kept_rows, kept_rows, 1)
    summed = own_part + swapped(handed, "expert", 0)
    returned = lax.all_to_all(
        summed.astype(jnp.bfloat16), "expert", split_axis=0, concat_axis=0, tiled=True
    )
    returned = returned.reshape(experts * capacity, out_columns)
    gathered = jnp.einsum("pt,pd->td", select, returned, preferred_element_type=jnp.float32)
    weights = codes[:, 0].astype(jnp.float32) / 1024.0
    return (weights[:, None] * gathered).astype(jnp.bfloat16)


def z_send(x, distance):
    size = lax.axis_size("expert")
    return lax.ppermute(x, "expert", [(i, i ^ distance) for i in range(size)])


def ring_send(x):
    size, cores = lax.axis_size("expert"), lax.axis_size("seq")
    pairs = [
        (i * cores + core, (i + step) % size * cores + core)
        for i in range(size)
        for core, step in enumerate((1, -1))
    ]
    return lax.ppermute(x, ("expert", "seq"), pairs)


def half(x, index):
    rows = x.shape[0] // 2
    return lax.dynamic_slice_in_dim(x, index * rows, rows, 0)


def in_order(own, other, index, axis=0):
    return jnp.where(
        index == 0,
        jnp.concatenate([own, other], axis),
        jnp.concatenate([other, own], axis),
    )


VMEM = pl.BlockSpec(memory_space=pltpu.VMEM)
SMEM = pl.BlockSpec(memory_space=pltpu.SMEM)
LIMIT = 48 * 1024 * 1024


def hidden_kernel(parts, index, *refs):
    taken, weights = refs[:parts], refs[parts : parts + 4]
    out, rows, blocks, acts, part_sems, block_sems = refs[parts + 4 :]
    share, depth = rows.shape[0] // parts, weights[0].shape[0]
    width = out.shape[1]
    step = depth // 2

    def part_copy(i):
        target = rows.at[pl.ds(i * share, share), :]
        return pltpu.make_async_copy(taken[i], target, part_sems.at[i])

    def block_copy(i, half):
        source = weights[2 * (i // 2) + half].at[pl.ds(i % 2 * step, step), :]
        return pltpu.make_async_copy(source, blocks.at[i, half], block_sems.at[i, half])

    for i in range(parts):
        part_copy(i).start()
    for i in range(4):
        for half in range(2):
            block_copy(i, half).start()
    for i in range(parts):
        part_copy(i).wait()
    for i in range(4):
        for half in range(2):
            block_copy(i, half).wait()
        value = jnp.dot(
            rows[:, i * step : (i + 1) * step],
            jnp.concatenate([blocks[i, 0], blocks[i, 1]], axis=1),
            preferred_element_type=jnp.float32,
        )
        if i == 0:
            acts[...] = value
        else:
            acts[...] += value

    gate_act, up_act = acts[:, :width], acts[:, width:]
    value = (jax.nn.silu(gate_act) * up_act).astype(out.dtype)
    out[pl.ds(pl.multiple_of(index[0] * share, share), share), :] = value[:share]
    out[pl.ds(pl.multiple_of((1 - index[0]) * share, share), share), :] = value[share:]


def hidden_call(index, parts, weights):
    depth, width = weights[0].shape
    rows = sum(part.shape[0] for part in parts)
    held = pl.BlockSpec(memory_space=pltpu.HBM)
    return pl.pallas_call(
        functools.partial(hidden_kernel, len(parts)),
        out_shape=jax.ShapeDtypeStruct((rows, width), jnp.bfloat16),
        in_specs=[SMEM] + [held] * (len(parts) + 4),
        out_specs=VMEM,
        scratch_shapes=[
            pltpu.VMEM((rows, 2 * depth), jnp.bfloat16),
            pltpu.VMEM((4, 2, depth // 2, width), jnp.bfloat16),
            pltpu.VMEM((rows, 2 * width), jnp.float32),
            pltpu.SemaphoreType.DMA((len(parts),)),
            pltpu.SemaphoreType.DMA((4, 2)),
        ],
        compiler_params=pltpu.CompilerParams(vmem_limit_bytes=LIMIT),
        cost_estimate=pl.CostEstimate(flops=0, bytes_accessed=0, transcendentals=0),
    )(index, *parts, *weights)


def ring(tokens, gate_weight, up_weight, down_weight, expert_ids, codes, expert_home):
    z, x, c = lax.axis_index("expert"), lax.axis_index("tensor"), lax.axis_index("seq")
    f32, bf16 = jnp.float32, jnp.bfloat16
    tied = lax.optimization_barrier
    odd = z % 2
    place = c ^ odd
    x_index = x.astype(jnp.int32).reshape(1)

    def to_tensor(part):
        return swapped(part, "tensor", 0)

    down = down_weight[0]
    own_half, given_half = half(tokens, c), half(tokens, 1 - c)
    own_rows = tied(jnp.concatenate([own_half, swapped(given_half, "seq", 0)], axis=1))
    moving, staying = tied((half(own_rows, x), half(own_rows, 1 - x)))
    block1 = ring_send(moving)
    gate_own, up_own, staying = tied((gate_weight[0], up_weight[0], staying))
    weights = (gate_own, up_own, swapped(gate_own, "seq", 0), swapped(up_own, "seq", 0))

    def activated(part, other):
        return hidden_call(x_index, (part, other), weights)

    def partial_out(own, other):
        both = in_order(own, other, x, 1)
        rows = in_order(both, swapped(both, "seq", 0), place)
        return jnp.dot(rows, down, preferred_element_type=f32)

    def a_half(part):
        return part[: part.shape[0] // 2]

    def b_half(part):
        return part[part.shape[0] // 2 :]

    def added(part, received):
        return (part + received.astype(f32)).astype(bf16)

    act0 = activated(moving, staying)
    hidden0 = to_tensor(act0)
    block1, act0, hidden0 = tied((block1, act0, hidden0))
    block2, other1 = ring_send(block1), to_tensor(block1)
    part0 = partial_out(act0, hidden0)
    block2, other1, part0 = tied((block2, other1, part0))
    block3, other2 = ring_send(block2), to_tensor(block2)
    act1 = activated(block1, other1)
    hidden1 = to_tensor(act1)
    block3, other2, hidden1 = tied((block3, other2, hidden1))
    other3 = to_tensor(block3)
    part1 = partial_out(act1, hidden1).astype(bf16)
    other2, part1 = tied((other2, part1))
    back1 = z_send(part1, 1)
    act2 = activated(block2, other2)
    hidden2 = to_tensor(act2)
    other3, act2 = tied((other3, act2))
    act3 = activated(block3, other3)
    act3, back1 = tied((act3, back1))
    hidden3 = to_tensor(act3)
    act3, hidden2 = tied((act3, hidden2))
    part2 = partial_out(act2, hidden2)
    part2, hidden3 = tied((part2, hidden3))
    sent_a2 = z_send(a_half(part2).astype(bf16), 1)
    home_b2 = z_send(added(b_half(part2), a_half(back1)), 2)
    part3 = partial_out(act3, hidden3)
    home_b3 = z_send(added(b_half(part3), sent_a2), 3)
    last_a, home_b2 = tied((a_half(part3).astype(bf16), home_b2))
    sent_a3 = z_send(last_a, 1)

    def in_rows(part_a, part_b):
        return in_order(part_a, part_b, odd)

    ids = expert_ids[:, 0]
    home = jnp.where(ids == 0, expert_home[0], expert_home[1])
    ours = (home == z // 2)[:, None]
    scale = codes[:, 0].astype(f32) / 1024.0
    from_pair = in_rows(a_half(part0) + b_half(back1).astype(f32), b_half(part0))
    from_others = in_rows(home_b3, home_b2).astype(f32)
    so_far = tied(jnp.where(ours, from_pair, from_others))
    last = in_rows(jnp.zeros_like(sent_a3), sent_a3).astype(f32)
    expert_out = (so_far + jnp.where(ours, last, 0.0)).astype(bf16)
    return (scale[:, None] * expert_out.astype(f32)).astype(bf16)


def local(*arguments):
    experts = arguments[-1].shape[0]
    sizes = tuple(lax.axis_size(axis) for axis in ("expert", "tensor", "seq"))
    if experts == 2 and sizes == (4, 2, 2):
        return ring(*arguments)
    return routed(*arguments)


def solution(mesh):
    in_specs = (
        P(("groups", "expert"), "seq"),
        P("expert", "seq", "tensor"),
        P("expert", "seq", "tensor"),
        P("expert", None, ("tensor", "seq")),
        P(("groups", "expert"), None),
        P(("groups", "expert"), None),
        P(),
    )
    out_specs = P(("groups", "expert"), ("tensor", "seq"))
    return jax.shard_map(local, mesh=mesh, in_specs=in_specs, out_specs=out_specs, check_vma=False)
```

```python
import functools

import jax
import jax.numpy as jnp
from jax import lax
from jax.experimental import pallas as pl
from jax.experimental.pallas import tpu as pltpu
from jax.sharding import PartitionSpec as P


def swapped(x, axis, distance):
    return lax.ppermute(x, axis, [(i, i ^ 1 << distance) for i in range(lax.axis_size(axis))])


def routed(tokens, gate_weight, up_weight, down_weight, expert_ids, codes, expert_home):
    tok_rows, columns_dev = tokens.shape
    experts = expert_home.shape[0]
    capacity = min(tok_rows, 2 * tok_rows // experts)
    owners = 2 * experts
    numbers = jnp.arange(experts, dtype=jnp.int32)
    chosen = (expert_ids == numbers[None, :]).astype(jnp.int32)
    home_slot = jnp.sum(chosen * expert_home[None, :], axis=1)
    onehot = (home_slot[:, None] == numbers[None, :]).astype(jnp.int32)
    before = jnp.cumsum(onehot, axis=0) - onehot
    position = jnp.sum(before * onehot, axis=1)
    target = home_slot * capacity + position
    select = (jnp.arange(experts * capacity, dtype=jnp.int32)[:, None] == target[None, :]).astype(
        jnp.bfloat16
    )
    packed = jnp.dot(select, tokens, preferred_element_type=jnp.float32).astype(jnp.bfloat16)
    packed = packed.reshape(experts, capacity, columns_dev)
    member = lax.axis_index("expert") % 2
    doubled = jnp.broadcast_to(packed[:, None], (experts, 2, capacity, columns_dev))
    doubled = doubled.reshape(owners, capacity, columns_dev)
    arrived = lax.all_to_all(doubled, "expert", split_axis=0, concat_axis=0, tiled=True)
    slot_count = owners * capacity
    received = arrived.reshape(slot_count, columns_dev)
    gate_part = jnp.dot(received, gate_weight[0], preferred_element_type=jnp.float32)
    up_part = jnp.dot(received, up_weight[0], preferred_element_type=jnp.float32)
    gate_act, up_act = lax.psum((gate_part, up_part), "seq")
    activated = (jax.nn.silu(gate_act) * up_act).astype(jnp.bfloat16)
    down_block = down_weight[0]
    out_columns = down_block.shape[1]
    partial_value = jnp.dot(
        lax.all_gather(activated, "tensor", axis=1, tiled=True),
        down_block,
        preferred_element_type=jnp.float32,
    )
    partial_value = partial_value.reshape(owners, capacity, out_columns)
    kept_rows = capacity // 2
    own_part = lax.dynamic_slice_in_dim(partial_value, member * kept_rows, kept_rows, 1)
    handed = lax.dynamic_slice_in_dim(partial_value, (1 - member) * kept_rows, kept_rows, 1)
    summed = own_part + swapped(handed, "expert", 0)
    returned = lax.all_to_all(
        summed.astype(jnp.bfloat16), "expert", split_axis=0, concat_axis=0, tiled=True
    )
    returned = returned.reshape(experts * capacity, out_columns)
    gathered = jnp.einsum("pt,pd->td", select, returned, preferred_element_type=jnp.float32)
    weights = codes[:, 0].astype(jnp.float32) / 1024.0
    return (weights[:, None] * gathered).astype(jnp.bfloat16)


def z_send(x, distance):
    size = lax.axis_size("expert")
    return lax.ppermute(x, "expert", [(i, i ^ distance) for i in range(size)])


def ring_send(x):
    size, cores = lax.axis_size("expert"), lax.axis_size("seq")
    pairs = [
        (i * cores + core, (i + step) % size * cores + core)
        for i in range(size)
        for core, step in enumerate((1, -1))
    ]
    return lax.ppermute(x, ("expert", "seq"), pairs)


def half(x, index):
    rows = x.shape[0] // 2
    return lax.dynamic_slice_in_dim(x, index * rows, rows, 0)


def in_order(own, other, index, axis=0):
    return jnp.where(
        index == 0,
        jnp.concatenate([own, other], axis),
        jnp.concatenate([other, own], axis),
    )


VMEM = pl.BlockSpec(memory_space=pltpu.VMEM)
SMEM = pl.BlockSpec(memory_space=pltpu.SMEM)
LIMIT = 48 * 1024 * 1024


def hidden_kernel(parts, index, *refs):
    taken, weights = refs[:parts], refs[parts : parts + 4]
    out, rows, blocks, acts, part_sems, block_sems = refs[parts + 4 :]
    share, depth = rows.shape[0] // parts, weights[0].shape[0]
    width = out.shape[1]
    step = depth // 2

    def part_copy(i):
        target = rows.at[pl.ds(i * share, share), :]
        return pltpu.make_async_copy(taken[i], target, part_sems.at[i])

    def block_copy(i, side):
        source = weights[2 * (i // 2) + side].at[pl.ds(i % 2 * step, step), :]
        return pltpu.make_async_copy(source, blocks.at[i, side], block_sems.at[i, side])

    for i in range(parts):
        part_copy(i).start()
    for i in range(4):
        for side in range(2):
            block_copy(i, side).start()
    for i in range(parts):
        part_copy(i).wait()
    for i in range(4):
        for side in range(2):
            block_copy(i, side).wait()
        value = jnp.dot(
            rows[:, i * step : (i + 1) * step],
            jnp.concatenate([blocks[i, 0], blocks[i, 1]], axis=1),
            preferred_element_type=jnp.float32,
        )
        if i == 0:
            acts[...] = value
        else:
            acts[...] += value

    gate_act, up_act = acts[:, :width], acts[:, width:]
    value = (jax.nn.silu(gate_act) * up_act).astype(out.dtype)
    half = out.shape[0] // 2
    out[pl.ds(pl.multiple_of(index[0] * half, half), half), :] = value[:half]
    out[pl.ds(pl.multiple_of((1 - index[0]) * half, half), half), :] = value[half:]


def hidden_call(index, parts, weights):
    depth, width = weights[0].shape
    rows = sum(part.shape[0] for part in parts)
    held = pl.BlockSpec(memory_space=pltpu.HBM)
    return pl.pallas_call(
        functools.partial(hidden_kernel, len(parts)),
        out_shape=jax.ShapeDtypeStruct((rows, width), jnp.bfloat16),
        in_specs=[SMEM] + [held] * (len(parts) + 4),
        out_specs=VMEM,
        scratch_shapes=[
            pltpu.VMEM((rows, 2 * depth), jnp.bfloat16),
            pltpu.VMEM((4, 2, depth // 2, width), jnp.bfloat16),
            pltpu.VMEM((rows, 2 * width), jnp.float32),
            pltpu.SemaphoreType.DMA((len(parts),)),
            pltpu.SemaphoreType.DMA((4, 2)),
        ],
        compiler_params=pltpu.CompilerParams(vmem_limit_bytes=LIMIT),
        cost_estimate=pl.CostEstimate(flops=0, bytes_accessed=0, transcendentals=0),
    )(index, *parts, *weights)


def ring(tokens, gate_weight, up_weight, down_weight, expert_ids, codes, expert_home):
    z, x, c = lax.axis_index("expert"), lax.axis_index("tensor"), lax.axis_index("seq")
    f32, bf16 = jnp.float32, jnp.bfloat16
    tied = lax.optimization_barrier
    odd = z % 2
    place = c ^ odd
    x_index = x.astype(jnp.int32).reshape(1)

    def to_tensor(part):
        return swapped(part, "tensor", 0)

    down = down_weight[0]
    own_half, given_half = half(tokens, c), half(tokens, 1 - c)
    own_rows = tied(jnp.concatenate([own_half, swapped(given_half, "seq", 0)], axis=1))
    moving, staying = tied((half(own_rows, x), half(own_rows, 1 - x)))
    first, second = tied(tuple(jnp.split(moving, 2)))
    block1a, block1b = ring_send(first), ring_send(second)
    gate_own, up_own, staying = tied((gate_weight[0], up_weight[0], staying))
    weights = (gate_own, up_own, swapped(gate_own, "seq", 0), swapped(up_own, "seq", 0))

    def activated(*parts):
        return hidden_call(x_index, parts, weights)

    def partial_out(own, other):
        both = in_order(own, other, x, 1)
        rows = in_order(both, swapped(both, "seq", 0), place)
        return jnp.dot(rows, down, preferred_element_type=f32)

    def a_half(part):
        return part[: part.shape[0] // 2]

    def b_half(part):
        return part[part.shape[0] // 2 :]

    def added(part, received):
        return (part + received.astype(f32)).astype(bf16)

    block2a, other1a = ring_send(block1a), to_tensor(block1a)
    act0 = activated(moving, staying)
    block1b, act0 = tied((block1b, act0))
    hidden0 = to_tensor(act0)
    block2b, other1b = ring_send(block1b), to_tensor(block1b)
    block2a, other1a = tied((block2a, other1a))
    block3a, other2a = ring_send(block2a), to_tensor(block2a)
    block2b, other1a, other1b = tied((block2b, other1a, other1b))
    block3b, other2b = ring_send(block2b), to_tensor(block2b)
    act1 = activated(block1a, block1b, other1a, other1b)
    act1, block3a, other2a = tied((act1, block3a, other2a))
    hidden1 = to_tensor(act1)
    other3a = to_tensor(block3a)
    block3b, hidden1, other2b = tied((block3b, hidden1, other2b))
    other3b = to_tensor(block3b)
    part1 = partial_out(act1, hidden1).astype(bf16)
    other2a, other2b, part1 = tied((other2a, other2b, part1))
    back1 = z_send(part1, 1)
    part0 = partial_out(act0, hidden0)
    act2 = activated(block2a, block2b, other2a, other2b)
    hidden2 = to_tensor(act2)
    other3a, other3b, act2, part0 = tied((other3a, other3b, act2, part0))
    act3 = activated(block3a, block3b, other3a, other3b)
    hidden3 = to_tensor(act3)
    act3, hidden2 = tied((act3, hidden2))
    part2 = partial_out(act2, hidden2)
    part2, hidden3, back1 = tied((part2, hidden3, back1))
    sent_a2 = z_send(a_half(part2).astype(bf16), 1)
    home_b2 = z_send(added(b_half(part2), a_half(back1)), 2)
    part3 = partial_out(act3, hidden3)
    home_b3 = z_send(added(b_half(part3), sent_a2), 3)
    last_a, home_b2 = tied((a_half(part3).astype(bf16), home_b2))
    sent_a3 = z_send(last_a, 1)

    def in_rows(part_a, part_b):
        return in_order(part_a, part_b, odd)

    ids = expert_ids[:, 0]
    home = jnp.where(ids == 0, expert_home[0], expert_home[1])
    ours = (home == z // 2)[:, None]
    scale = codes[:, 0].astype(f32) / 1024.0
    from_pair = in_rows(a_half(part0) + b_half(back1).astype(f32), b_half(part0))
    from_others = in_rows(home_b3, home_b2).astype(f32)
    so_far = tied(jnp.where(ours, from_pair, from_others))
    last = in_rows(jnp.zeros_like(sent_a3), sent_a3).astype(f32)
    expert_out = (so_far + jnp.where(ours, last, 0.0)).astype(bf16)
    return (scale[:, None] * expert_out.astype(f32)).astype(bf16)


def local(*arguments):
    experts = arguments[-1].shape[0]
    sizes = tuple(lax.axis_size(axis) for axis in ("expert", "tensor", "seq"))
    if experts == 2 and sizes == (4, 2, 2):
        return ring(*arguments)
    return routed(*arguments)


def solution(mesh):
    in_specs = (
        P(("groups", "expert"), "seq"),
        P("expert", "seq", "tensor"),
        P("expert", "seq", "tensor"),
        P("expert", None, ("tensor", "seq")),
        P(("groups", "expert"), None),
        P(("groups", "expert"), None),
        P(),
    )
    out_specs = P(("groups", "expert"), ("tensor", "seq"))
    return jax.shard_map(local, mesh=mesh, in_specs=in_specs, out_specs=out_specs, check_vma=False)
```

```python
import functools

import jax
import jax.numpy as jnp
from jax import lax
from jax.experimental import pallas as pl
from jax.experimental.pallas import tpu as pltpu
from jax.sharding import PartitionSpec as P


def swapped(x, axis, distance):
    return lax.ppermute(x, axis, [(i, i ^ 1 << distance) for i in range(lax.axis_size(axis))])


def routed(tokens, gate_weight, up_weight, down_weight, expert_ids, codes, expert_home):
    tok_rows, columns_dev = tokens.shape
    experts = expert_home.shape[0]
    capacity = min(tok_rows, 2 * tok_rows // experts)
    owners = 2 * experts
    numbers = jnp.arange(experts, dtype=jnp.int32)
    chosen = (expert_ids == numbers[None, :]).astype(jnp.int32)
    home_slot = jnp.sum(chosen * expert_home[None, :], axis=1)
    onehot = (home_slot[:, None] == numbers[None, :]).astype(jnp.int32)
    before = jnp.cumsum(onehot, axis=0) - onehot
    position = jnp.sum(before * onehot, axis=1)
    target = home_slot * capacity + position
    select = (jnp.arange(experts * capacity, dtype=jnp.int32)[:, None] == target[None, :]).astype(
        jnp.bfloat16
    )
    packed = jnp.dot(select, tokens, preferred_element_type=jnp.float32).astype(jnp.bfloat16)
    packed = packed.reshape(experts, capacity, columns_dev)
    member = lax.axis_index("expert") % 2
    doubled = jnp.broadcast_to(packed[:, None], (experts, 2, capacity, columns_dev))
    doubled = doubled.reshape(owners, capacity, columns_dev)
    arrived = lax.all_to_all(doubled, "expert", split_axis=0, concat_axis=0, tiled=True)
    slot_count = owners * capacity
    received = arrived.reshape(slot_count, columns_dev)
    gate_part = jnp.dot(received, gate_weight[0], preferred_element_type=jnp.float32)
    up_part = jnp.dot(received, up_weight[0], preferred_element_type=jnp.float32)
    gate_act, up_act = lax.psum((gate_part, up_part), "seq")
    activated = (jax.nn.silu(gate_act) * up_act).astype(jnp.bfloat16)
    down_block = down_weight[0]
    out_columns = down_block.shape[1]
    partial_value = jnp.dot(
        lax.all_gather(activated, "tensor", axis=1, tiled=True),
        down_block,
        preferred_element_type=jnp.float32,
    )
    partial_value = partial_value.reshape(owners, capacity, out_columns)
    kept_rows = capacity // 2
    own_part = lax.dynamic_slice_in_dim(partial_value, member * kept_rows, kept_rows, 1)
    handed = lax.dynamic_slice_in_dim(partial_value, (1 - member) * kept_rows, kept_rows, 1)
    summed = own_part + swapped(handed, "expert", 0)
    returned = lax.all_to_all(
        summed.astype(jnp.bfloat16), "expert", split_axis=0, concat_axis=0, tiled=True
    )
    returned = returned.reshape(experts * capacity, out_columns)
    gathered = jnp.einsum("pt,pd->td", select, returned, preferred_element_type=jnp.float32)
    weights = codes[:, 0].astype(jnp.float32) / 1024.0
    return (weights[:, None] * gathered).astype(jnp.bfloat16)


def z_send(x, distance):
    size = lax.axis_size("expert")
    return lax.ppermute(x, "expert", [(i, i ^ distance) for i in range(size)])


def ring_send(x):
    size, cores = lax.axis_size("expert"), lax.axis_size("seq")
    pairs = [
        (i * cores + core, (i + step) % size * cores + core)
        for i in range(size)
        for core, step in enumerate((1, -1))
    ]
    return lax.ppermute(x, ("expert", "seq"), pairs)


def half(x, index):
    rows = x.shape[0] // 2
    return lax.dynamic_slice_in_dim(x, index * rows, rows, 0)


def in_order(own, other, index, axis=0):
    return jnp.where(
        index == 0,
        jnp.concatenate([own, other], axis),
        jnp.concatenate([other, own], axis),
    )


VMEM = pl.BlockSpec(memory_space=pltpu.VMEM)
SMEM = pl.BlockSpec(memory_space=pltpu.SMEM)
LIMIT = 48 * 1024 * 1024


def hidden_kernel(parts, index, *refs):
    taken, weights = refs[:parts], refs[parts : parts + 4]
    out, rows, blocks, acts, part_sems, block_sems = refs[parts + 4 :]
    share, depth = rows.shape[0] // parts, weights[0].shape[0]
    width = out.shape[1]
    step = depth // 2

    def part_copy(i):
        target = rows.at[pl.ds(i * share, share), :]
        return pltpu.make_async_copy(taken[i], target, part_sems.at[i])

    def block_copy(i, side):
        source = weights[2 * (i // 2) + side].at[pl.ds(i % 2 * step, step), :]
        return pltpu.make_async_copy(source, blocks.at[i, side], block_sems.at[i, side])

    for i in range(parts):
        part_copy(i).start()
    for i in range(4):
        for side in range(2):
            block_copy(i, side).start()
    for i in range(parts):
        part_copy(i).wait()
    for i in range(4):
        for side in range(2):
            block_copy(i, side).wait()
        value = jnp.dot(
            rows[:, i * step : (i + 1) * step],
            jnp.concatenate([blocks[i, 0], blocks[i, 1]], axis=1),
            preferred_element_type=jnp.float32,
        )
        if i == 0:
            acts[...] = value
        else:
            acts[...] += value

    gate_act, up_act = acts[:, :width], acts[:, width:]
    value = (jax.nn.silu(gate_act) * up_act).astype(out.dtype)
    half = out.shape[0] // 2
    out[pl.ds(pl.multiple_of(index[0] * half, half), half), :] = value[:half]
    out[pl.ds(pl.multiple_of((1 - index[0]) * half, half), half), :] = value[half:]


def hidden_call(index, parts, weights):
    depth, width = weights[0].shape
    rows = sum(part.shape[0] for part in parts)
    held = pl.BlockSpec(memory_space=pltpu.HBM)
    return pl.pallas_call(
        functools.partial(hidden_kernel, len(parts)),
        out_shape=jax.ShapeDtypeStruct((rows, width), jnp.bfloat16),
        in_specs=[SMEM] + [held] * (len(parts) + 4),
        out_specs=VMEM,
        scratch_shapes=[
            pltpu.VMEM((rows, 2 * depth), jnp.bfloat16),
            pltpu.VMEM((4, 2, depth // 2, width), jnp.bfloat16),
            pltpu.VMEM((rows, 2 * width), jnp.float32),
            pltpu.SemaphoreType.DMA((len(parts),)),
            pltpu.SemaphoreType.DMA((4, 2)),
        ],
        compiler_params=pltpu.CompilerParams(vmem_limit_bytes=LIMIT),
        cost_estimate=pl.CostEstimate(flops=0, bytes_accessed=0, transcendentals=0),
    )(index, *parts, *weights)


def ring(tokens, gate_weight, up_weight, down_weight, expert_ids, codes, expert_home):
    z, x, c = lax.axis_index("expert"), lax.axis_index("tensor"), lax.axis_index("seq")
    f32, bf16 = jnp.float32, jnp.bfloat16
    tied = lax.optimization_barrier
    odd = z % 2
    place = c ^ odd
    x_index = x.astype(jnp.int32).reshape(1)

    def to_tensor(part):
        return swapped(part, "tensor", 0)

    down = down_weight[0]
    own_half, given_half = half(tokens, c), half(tokens, 1 - c)
    own_rows = tied(jnp.concatenate([own_half, swapped(given_half, "seq", 0)], axis=1))
    moving, staying = tied((half(own_rows, x), half(own_rows, 1 - x)))
    first, second = tied(tuple(jnp.split(moving, 2)))
    block1a, block1b = ring_send(first), ring_send(second)
    gate_own, up_own, staying = tied((gate_weight[0], up_weight[0], staying))
    weights = (gate_own, up_own, swapped(gate_own, "seq", 0), swapped(up_own, "seq", 0))

    def activated(*parts):
        return hidden_call(x_index, parts, weights)

    def partial_out(own, other):
        both = in_order(own, other, x, 1)
        rows = in_order(both, swapped(both, "seq", 0), place)
        return jnp.dot(rows, down, preferred_element_type=f32)

    def a_half(part):
        return part[: part.shape[0] // 2]

    def b_half(part):
        return part[part.shape[0] // 2 :]

    def added(part, received):
        return (part + received.astype(f32)).astype(bf16)

    block2a, other1a = ring_send(block1a), to_tensor(block1a)
    act0 = activated(moving, staying)
    block1b, act0 = tied((block1b, act0))
    hidden0 = to_tensor(act0)
    block2b, other1b = ring_send(block1b), to_tensor(block1b)
    block2a, other1a = tied((block2a, other1a))
    block3a, other2a = ring_send(block2a), to_tensor(block2a)
    block2b, other1a, other1b = tied((block2b, other1a, other1b))
    block3b, other2b = ring_send(block2b), to_tensor(block2b)
    act1 = activated(block1a, block1b, other1a, other1b)
    act1, block3a, other2a = tied((act1, block3a, other2a))
    hidden1 = to_tensor(act1)
    other3a = to_tensor(block3a)
    block3b, hidden1, other2b = tied((block3b, hidden1, other2b))
    other3b = to_tensor(block3b)
    part1 = partial_out(act1, hidden1).astype(bf16)
    other2a, other2b, part1 = tied((other2a, other2b, part1))
    back1 = z_send(part1, 1)
    part0 = partial_out(act0, hidden0)
    act2 = activated(block2a, block2b, other2a, other2b)
    hidden2 = to_tensor(act2)
    other3a, other3b, act2, part0 = tied((other3a, other3b, act2, part0))
    act3 = activated(block3a, block3b, other3a, other3b)
    hidden3 = to_tensor(act3)
    act3, hidden2 = tied((act3, hidden2))
    part2 = partial_out(act2, hidden2)
    part2, hidden3, back1 = tied((part2, hidden3, back1))
    sent_a2 = z_send(a_half(part2).astype(bf16), 1)
    home_b2 = z_send(added(b_half(part2), a_half(back1)), 2)
    part3 = partial_out(act3, hidden3)
    home_b3 = z_send(added(b_half(part3), sent_a2), 3)
    last_a, home_b2 = tied((a_half(part3).astype(bf16), home_b2))
    sent_a3 = z_send(last_a, 1)

    def in_rows(part_a, part_b):
        return in_order(part_a, part_b, odd)

    ids = expert_ids[:, 0]
    home = jnp.where(ids == 0, expert_home[0], expert_home[1])
    ours = (home == z // 2)[:, None]
    scale = codes[:, 0].astype(f32) / 1024.0
    from_pair = in_rows(
        a_half(part0) + b_half(back1).astype(f32), b_half(part0) + sent_a3.astype(f32)
    )
    from_others = in_rows(home_b3, home_b2).astype(f32)
    expert_out = jnp.where(ours, from_pair, from_others).astype(bf16)
    return (scale[:, None] * expert_out.astype(f32)).astype(bf16)


def local(*arguments):
    experts = arguments[-1].shape[0]
    sizes = tuple(lax.axis_size(axis) for axis in ("expert", "tensor", "seq"))
    if experts == 2 and sizes == (4, 2, 2):
        return ring(*arguments)
    return routed(*arguments)


def solution(mesh):
    in_specs = (
        P(("groups", "expert"), "seq"),
        P("expert", "seq", "tensor"),
        P("expert", "seq", "tensor"),
        P("expert", None, ("tensor", "seq")),
        P(("groups", "expert"), None),
        P(("groups", "expert"), None),
        P(),
    )
    out_specs = P(("groups", "expert"), ("tensor", "seq"))
    return jax.shard_map(local, mesh=mesh, in_specs=in_specs, out_specs=out_specs, check_vma=False)
```
